32 devices in a mesh: group: 4 (over y, core), inner: 8 (over z, x).
Axes of the slice: x: 2, y: 2, z: 4, core: 2. Of those that a mesh axis runs over, the one named last changes fastest.
Arguments:
- left_part: bfloat16 [32768, 256], P(('group', 'inner')), may hold values from -12 to 12
- right_part: bfloat16 [32768, 256], P(('group', 'inner')), may hold values from -12 to 12
- relation: bfloat16 [256, 256], replicated, may hold values from -0.19 to 1.19
- src_index: int32 [32, 4, 512], P(('group', 'inner')), may hold values from 0 to 1023
- dst_index: int32 [32, 4, 512], P(('group', 'inner')), may hold values from 0 to 1023
- lengths: int32 [32, 4], P(('group', 'inner')), may hold values from 1 to 512, 1280 in all within a row
Outputs:
- left_out: bfloat16 [32768, 256], P(('group', 'inner'))
- right_out: bfloat16 [32768, 256], P(('group', 'inner'))
- relation_out: float32 [256, 256], replicated
The draws below stay inside these ranges and needn't reach their ends.
All inputs are finite; a program needn't handle non-finite values.
Results may differ from the reference program's by a relative error of at most 0.012.
The reference program's roundings to bfloat16 on the way (of `holding`, `picked`, `queries`, `coeffs` and `query_grad`) count: a program that leaves them out, or rounds other values in their place, can miss the bound.
Values may be sent and summed in bfloat16 or wider, within the bound.
A program may use at most 64 MiB of HBM per device.

```python
import math
import jax
import jax.numpy as jnp
import numpy as np
from jax import lax

D = 256
P_SIZE = 1024
E = 512
MEETINGS = 4
PARTS_SIZE = 32
N_GROUP = 4
N_INNER = 8


def embed_base(key, salt):
    normal_draw = jnp.clip(jax.random.normal(jax.random.fold_in(key, salt), (PARTS_SIZE * P_SIZE, D), jnp.float32), -6.0, 6.0)
    return normal_draw


def draw_left_part(key, part):
    values = embed_base(key, 1)
    return jnp.clip(values, -12.0, 12.0).astype(jnp.bfloat16)


def draw_right_part(key, part):
    values = embed_base(key, 2)
    return jnp.clip(values, -12.0, 12.0).astype(jnp.bfloat16)


def draw_relation(key, part):
    normal_draw = jnp.clip(jax.random.normal(jax.random.fold_in(key, 3), (D, D), jnp.float32), -6.0, 6.0) * (0.5 * D ** (-0.5))
    positions = jnp.arange(D)
    identity = (positions[:, None] == positions[None, :]).astype(jnp.float32)
    return (identity + normal_draw).astype(jnp.bfloat16)


def place_ends(drawn, own_key, least, high):
    longest = drawn.shape.index(max(drawn.shape))
    spots = []
    for shift in (0, 1):
        where = [jax.random.randint(jax.random.fold_in(own_key, axis), (), 0, length) for axis, length in enumerate(drawn.shape)]
        where[longest] = (where[longest] + shift) % drawn.shape[longest]
        spots.append(tuple(where))
    return drawn.at[spots[0]].set(least).at[spots[1]].set(high)


def length_profile(number_of, total, limit, slope):
    weights = [(1 << 20) // math.isqrt(rank ** slope) + 1 for rank in range(2, number_of + 1)]
    spare, counts = total - limit - (number_of - 1), [1] * (number_of - 1)
    while spare > 0:
        candidates = [i for i in range(number_of - 1) if counts[i] < limit]
        mass, budget = sum([weights[i] for i in candidates]), spare
        for i in candidates:
            more = min(limit - counts[i], max(1, budget * weights[i] // mass), spare)
            counts[i] = counts[i] + more
            spare = spare - more
    return np.array([limit] + counts)


def uneven_parts(key, number_of, total, reach, skew):
    if number_of == 2:
        one = jax.random.randint(key, (), max(1, total - reach), min(reach, total - 1) + 1)
        return jnp.stack([one, total - one])
    tallies = jnp.asarray(length_profile(number_of, total, reach, skew), jnp.int32)
    pairs = (number_of - 1) // 2
    donor, sink = tallies[1:1 + 2 * pairs:2], tallies[2:2 + 2 * pairs:2]
    slack = jnp.minimum(donor - 1, reach - sink)
    passed = jax.random.randint(jax.random.fold_in(key, 1), (pairs,), 0, 1 << 20) % (slack + 1)
    tallies = tallies.at[1:1 + 2 * pairs:2].set(donor - passed).at[2:2 + 2 * pairs:2].set(sink + passed)
    return tallies[jax.random.permutation(jax.random.fold_in(key, 2), number_of)]


def setup_inputs(seed: int = 0) -> dict:
    key_of = jax.random.split(jax.random.key(seed), 7)
    return {
        "left_part": draw_left_part(jax.random.fold_in(key_of[6], 71), 0),
        "right_part": draw_right_part(jax.random.fold_in(key_of[6], 71), 0),
        "relation": draw_relation(jax.random.fold_in(key_of[6], 71), 0),
        "src_index": place_ends(jax.random.randint(key_of[3], (PARTS_SIZE, MEETINGS, E), 0, P_SIZE), jax.random.fold_in(key_of[3], 1), 0, P_SIZE - 1).astype(jnp.int32),
        "dst_index": place_ends(jax.random.randint(key_of[4], (PARTS_SIZE, MEETINGS, E), 0, P_SIZE), jax.random.fold_in(key_of[4], 1), 0, P_SIZE - 1).astype(jnp.int32),
        "lengths": jax.vmap(lambda own: uneven_parts(own, MEETINGS, 5 * E // 2, E, 2))(jax.random.split(key_of[5], PARTS_SIZE)).reshape((PARTS_SIZE, MEETINGS)).astype(jnp.int32),
    }


SCORE_SCALE = 0.1875
LR_EMBED = 0.5
LR_RELATION = 0.02


def bucket(left_block, holding, relation, src_row, dst_row, length):
    picked = jnp.take(left_block, src_row, axis=0)
    queries = jnp.dot(picked, relation, preferred_element_type=jnp.float32).astype(jnp.bfloat16)
    scores = lax.dot_general(queries, holding, (((1,), (1,)), ((), ())), preferred_element_type=jnp.float32) * SCORE_SCALE
    maxima = jnp.max(scores, axis=1, keepdims=True)
    expos = jnp.exp(scores - maxima)
    softmax_w = expos / jnp.sum(expos, axis=1, keepdims=True)
    slot_ids = jnp.arange(src_row.shape[0], dtype=jnp.int32)
    live_mask = (slot_ids < length).astype(jnp.float32)
    columns = jnp.arange(holding.shape[0], dtype=jnp.int32)
    target = (columns[None, :] == dst_row[:, None]).astype(jnp.float32)
    coeffs = ((softmax_w - target) * live_mask[:, None]).astype(jnp.bfloat16)
    held_grad = lax.dot_general(coeffs, queries, (((0,), (0,)), ((), ())), preferred_element_type=jnp.float32) * SCORE_SCALE
    query_grad = (jnp.dot(coeffs, holding, preferred_element_type=jnp.float32) * SCORE_SCALE).astype(jnp.bfloat16)
    relation_grad = lax.dot_general(picked, query_grad, (((0,), (0,)), ((), ())), preferred_element_type=jnp.float32)
    row_grad = lax.dot_general(query_grad, relation, (((1,), (1,)), ((), ())), preferred_element_type=jnp.float32)
    left_grad = jax.ops.segment_sum(row_grad, src_row, num_segments=left_block.shape[0])
    new_left = (left_block.astype(jnp.float32) - LR_EMBED * left_grad).astype(jnp.bfloat16)
    new_holding = (holding.astype(jnp.float32) - LR_EMBED * held_grad).astype(jnp.bfloat16)
    return new_left, new_holding, relation_grad


def reference(left_part, right_part, relation, src_index, dst_index, lengths):
    part_count = N_GROUP * N_INNER
    log_inner = N_INNER.bit_length() - 1
    left_blocks = left_part.reshape(part_count, P_SIZE, D)
    holding = right_part.reshape(part_count, P_SIZE, D)
    part_ids = jnp.arange(part_count, dtype=jnp.int32)
    grad_total = jnp.zeros((D, D), jnp.float32)
    for meeting in range(MEETINGS):
        partner_ids = jnp.bitwise_xor(part_ids, jnp.int32(1 << (meeting % log_inner)))
        holding = jnp.take(holding, partner_ids, axis=0)

        def one_bucket(items):
            return bucket(items[0], items[1], relation, items[2], items[3], items[4])

        left_blocks, holding, grads = lax.map(one_bucket, (left_blocks, holding, src_index[:, meeting], dst_index[:, meeting], lengths[:, meeting]))
        grad_total = grad_total + jnp.sum(grads, axis=0)
    relation_out = relation.astype(jnp.float32) - LR_RELATION * grad_total
    return left_blocks.reshape(part_count * P_SIZE, D), holding.reshape(part_count * P_SIZE, D), relation_out
```

```python
import jax
import jax.numpy as jnp
from jax import lax
from jax.experimental import pallas as pl
from jax.experimental.pallas import tpu as pltpu
from jax.sharding import PartitionSpec as P

MEETINGS = 4

SCORE_SCALE = 0.1875
LR_EMBED = 0.5
LR_RELATION = 0.02

MESH = pl.DeviceIdType.MESH
F32 = jnp.float32
BF16 = jnp.bfloat16

ROW_CHUNKS = 4
EDGE_CHUNKS = 2


def partner(index, mask):
    return index + mask * (1 - 2 * lax.rem(lax.div(index, mask), 2))


def dot(a, b, a_dim, b_dim):
    return lax.dot_general(a, b, (((a_dim,), (b_dim,)), ((), ())), preferred_element_type=F32)


def kernel(
    n_inner,
    n_group,
    left_ref,
    right_ref,
    rel_ref,
    src_ref,
    dst_ref,
    len_ref,
    left_out,
    right_out,
    rel_out,
    met0,
    met1,
    met2,
    own2,
    next3,
    picked,
    query,
    query_in1,
    query_in2,
    grad_out1,
    grad_in1,
    coeffs,
    onehot,
    meta,
    meta_in1,
    meta_in3,
    part,
    part_in,
    shard,
    shard_in,
    gathered,
    move0_send,
    move0_recv,
    move2_send,
    move2_recv,
    move3_send,
    move3_recv,
    small_send,
    small_recv,
    rs_send,
    rs_recv,
    ar_send,
    ar_recv,
    ag_send,
    ag_recv,
):
    me = lax.axis_index("inner")
    my_group = lax.axis_index("group")
    rows, _ = left_ref.shape
    slots = src_ref.shape[2]
    log_inner = n_inner.bit_length() - 1
    masks = [2 ** (m % log_inner) for m in range(MEETINGS)]
    first = partner(me, masks[0])
    second = partner(me, masks[1])
    third = partner(second, masks[2])
    fourth = partner(me, masks[3])
    chunk = rows // ROW_CHUNKS
    width = slots // EDGE_CHUNKS

    def inner_id(index):
        return (my_group, index)

    def group_id(index):
        return (index, me)

    def remote(src, dst, send, recv, device):
        return pltpu.make_async_remote_copy(
            src_ref=src, dst_ref=dst, send_sem=send, recv_sem=recv, device_id=device, device_id_type=MESH
        )

    def piece(i):
        return pl.ds(i * chunk, chunk)

    barrier = pltpu.get_barrier_semaphore()
    for step in range(1, n_inner):
        pl.semaphore_signal(
            barrier, inc=1, device_id=inner_id(lax.rem(me + step, n_inner)), device_id_type=MESH
        )
    for step in range(1, n_group):
        pl.semaphore_signal(
            barrier, inc=1, device_id=group_id(lax.rem(my_group + step, n_group)), device_id_type=MESH
        )
    pl.semaphore_wait(barrier, n_inner + n_group - 2)

    move0 = [
        remote(right_ref.at[piece(i)], met0.at[piece(i)], move0_send.at[i], move0_recv.at[i], inner_id(first))
        for i in range(ROW_CHUNKS)
    ]
    for copy in move0:
        copy.start()

    slot_ids = lax.broadcasted_iota(jnp.int32, (1, slots), 1)
    meta[...] = jnp.zeros_like(meta)
    for m in range(MEETINGS):
        meta[m : m + 1, :] = jnp.where(slot_ids < len_ref[0:1, m : m + 1], dst_ref[0, m : m + 1, :], -1)
    meta1 = remote(meta, meta_in1, small_send.at[0], small_recv.at[0], inner_id(second))
    meta3 = remote(meta, meta_in3, small_send.at[1], small_recv.at[1], inner_id(fourth))
    meta1.start()
    meta3.start()

    entity = lax.broadcasted_iota(jnp.int32, (rows, width), 0)

    def columns(i):
        return slice(i * width, (i + 1) * width)

    def make_queries(m, table):
        for i in range(EDGE_CHUNKS):
            hot = (entity == src_ref[0, m : m + 1, columns(i)]).astype(F32).astype(BF16)
            onehot[:, columns(i)] = hot
            chosen = dot(table, hot, 0, 0).astype(BF16)
            picked[:, columns(i)] = chosen
            query[m, :, columns(i)] = dot(rel_ref[...], chosen, 0, 0).astype(BF16)

    def make_coeffs(holding, asked, targets):
        for i in range(EDGE_CHUNKS):
            scores = dot(holding, asked[:, columns(i)], 1, 0) * SCORE_SCALE
            expos = jnp.exp(scores - jnp.max(scores, axis=0, keepdims=True))
            weight = expos * (1.0 / jnp.sum(expos, axis=0, keepdims=True))
            target = targets[:, columns(i)]
            weight = weight - (entity == target).astype(F32)
            weight = weight * (target >= 0).astype(F32)
            coeffs[:, columns(i)] = weight.astype(BF16)

    def query_grad(holding):
        return (dot(holding, coeffs[...], 0, 0) * SCORE_SCALE).astype(BF16)

    def held_update(holding, asked, i):
        held_grad = dot(coeffs[piece(i), :], asked, 1, 1) * SCORE_SCALE
        return (holding.astype(F32) - LR_EMBED * held_grad).astype(BF16)

    def left_update(table, grad):
        row_grad = dot(rel_ref[...], grad, 1, 0)
        high = row_grad.astype(BF16)
        low = (row_grad - high.astype(F32)).astype(BF16)
        hot = onehot[...]
        left_grad = dot(hot, high, 1, 1) + dot(hot, low, 1, 1)
        return (table.astype(F32) - LR_EMBED * left_grad).astype(BF16)

    def relation_grad(grad):
        return dot(picked[...], grad, 1, 1)

    make_queries(0, left_ref[...])
    for copy in move0:
        copy.wait()
    make_coeffs(met0[...], query[0], meta[0:1, :])
    grad = query_grad(met0[...])
    total = relation_grad(grad)
    left_out[...] = left_update(left_ref[...], grad)
    make_queries(1, left_out[...])
    ask1 = remote(query.at[1], query_in1, small_send.at[2], small_recv.at[2], inner_id(second))
    ask1.start()
    for i in range(ROW_CHUNKS):
        met1[piece(i), :] = held_update(met0[piece(i), :], query[0], i)

    meta1.wait()
    ask1.wait()
    make_coeffs(met1[...], query_in1[...], meta_in1[1:2, :])
    move2 = [
        remote(met2.at[piece(i)], own2.at[piece(i)], move2_send.at[i], move2_recv.at[i], inner_id(third))
        for i in range(ROW_CHUNKS)
    ]
    grad_out1[...] = query_grad(met1[...])
    back1 = remote(grad_out1, grad_in1, small_send.at[3], small_recv.at[3], inner_id(second))
    back1.start()
    for i in range(ROW_CHUNKS):
        met2[piece(i), :] = held_update(met1[piece(i), :], query_in1[...], i)
        move2[i].start()
    back1.wait()
    grad = grad_in1[...]
    total = total + relation_grad(grad)
    left_out[...] = left_update(left_out[...], grad)

    make_queries(2, left_out[...])
    ask2 = remote(query.at[2], query_in2, small_send.at[4], small_recv.at[4], inner_id(fourth))
    ask2.start()
    move3 = [
        remote(own2.at[piece(i)], next3.at[piece(i)], move3_send.at[i], move3_recv.at[i], inner_id(fourth))
        for i in range(ROW_CHUNKS)
    ]
    for i in range(ROW_CHUNKS):
        move2[i].wait()
        move3[i].start()
    make_coeffs(own2[...], query[2], meta[2:3, :])
    grad = query_grad(own2[...])
    total = total + relation_grad(grad)
    left_out[...] = left_update(left_out[...], grad)
    make_queries(3, left_out[...])
    meta3.wait()
    ask2.wait()
    for copy in move3:
        copy.wait()
    make_coeffs(next3[...], query_in2[...], meta_in3[2:3, :])
    for i in range(ROW_CHUNKS):
        right_out[piece(i), :] = held_update(next3[piece(i), :], query_in2[...], i)

    make_coeffs(right_out[...], query[3], meta[3:4, :])
    grad = query_grad(right_out[...])
    total = total + relation_grad(grad)

    share = rel_ref.shape[0] // n_inner
    for i in range(n_inner):
        part[i] = total[i * share : (i + 1) * share, :].astype(BF16)
    scatter = []
    for step in range(1, n_inner):
        to = lax.rem(me + step, n_inner)
        copy = remote(
            part.at[to], part_in.at[step - 1], rs_send.at[step - 1], rs_recv.at[step - 1], inner_id(to)
        )
        copy.start()
        scatter.append(copy)
    for i in range(ROW_CHUNKS):
        right_out[piece(i), :] = held_update(right_out[piece(i), :], query[3], i)
    left_out[...] = left_update(left_out[...], grad)
    own = part[me].astype(F32)
    for step, copy in enumerate(scatter):
        copy.wait()
        own = own + part_in[step].astype(F32)
    shard[...] = own
    everyone = []
    for step in range(1, n_group):
        to = lax.rem(my_group + step, n_group)
        copy = remote(
            shard, shard_in.at[my_group], ar_send.at[step - 1], ar_recv.at[step - 1], group_id(to)
        )
        copy.start()
        everyone.append(copy)
    shard_in[my_group] = own
    for copy in everyone:
        copy.wait()
    whole = shard_in[0]
    for g in range(1, n_group):
        whole = whole + shard_in[g]
    gathered[me] = whole.astype(BF16)
    spread = []
    for step in range(1, n_inner):
        to = lax.rem(me + step, n_inner)
        copy = remote(
            gathered.at[me], gathered.at[me], ag_send.at[step - 1], ag_recv.at[step - 1], inner_id(to)
        )
        copy.start()
        spread.append(copy)
    for copy in spread:
        copy.wait()
    for i in range(n_inner):
        here = slice(i * share, (i + 1) * share)
        rel_out[here, :] = rel_ref[here, :].astype(F32) - LR_RELATION * gathered[i].astype(F32)


def shards(left_part, right_part, relation, src_index, dst_index, lengths):
    n_inner = lax.axis_size("inner")
    n_group = lax.axis_size("group")
    rows, depth = left_part.shape
    slots = src_index.shape[2]
    share = depth // n_inner
    block = pltpu.VMEM((rows, depth), BF16)
    asked = pltpu.VMEM((depth, slots), BF16)
    meta = pltpu.VMEM((2 * MEETINGS, slots), jnp.int32)
    dma = pltpu.SemaphoreType.DMA
    vmem = pl.BlockSpec(memory_space=pltpu.VMEM)

    def body(*refs):
        kernel(n_inner, n_group, *refs)

    return pl.pallas_call(
        body,
        out_shape=(
            jax.ShapeDtypeStruct((rows, depth), BF16),
            jax.ShapeDtypeStruct((rows, depth), BF16),
            jax.ShapeDtypeStruct((depth, depth), F32),
        ),
        in_specs=[vmem] * 6,
        out_specs=(vmem,) * 3,
        scratch_shapes=[
            block,
            block,
            block,
            block,
            block,
            asked,
            pltpu.VMEM((MEETINGS, depth, slots), BF16),
            asked,
            asked,
            asked,
            asked,
            pltpu.VMEM((rows, slots), BF16),
            pltpu.VMEM((rows, slots), BF16),
            meta,
            meta,
            meta,
            pltpu.VMEM((n_inner, share, depth), BF16),
            pltpu.VMEM((n_inner - 1, share, depth), BF16),
            pltpu.VMEM((share, depth), F32),
            pltpu.VMEM((n_group, share, depth), F32),
            pltpu.VMEM((n_inner, share, depth), BF16),
            dma((ROW_CHUNKS,)),
            dma((ROW_CHUNKS,)),
            dma((ROW_CHUNKS,)),
            dma((ROW_CHUNKS,)),
            dma((ROW_CHUNKS,)),
            dma((ROW_CHUNKS,)),
            dma((5,)),
            dma((5,)),
            dma((n_inner - 1,)),
            dma((n_inner - 1,)),
            dma((n_group - 1,)),
            dma((n_group - 1,)),
            dma((n_inner - 1,)),
            dma((n_inner - 1,)),
        ],
        compiler_params=pltpu.CompilerParams(
            collective_id=0, has_side_effects=True, vmem_limit_bytes=48 * 1024 * 1024
        ),
        cost_estimate=pl.CostEstimate(
            flops=MEETINGS * 12 * rows * slots * depth,
            bytes_accessed=8 * rows * depth,
            transcendentals=MEETINGS * rows * slots,
        ),
        name="bucket_meetings",
    )(left_part, right_part, relation, src_index, dst_index, lengths)


def solution(mesh):
    in_specs = (
        P(("group", "inner"), None),
        P(("group", "inner"), None),
        P(),
        P(("group", "inner"), None, None),
        P(("group", "inner"), None, None),
        P(("group", "inner"), None),
    )
    out_specs = (P(("group", "inner"), None), P(("group", "inner"), None), P())
    return jax.shard_map(shards, mesh=mesh, in_specs=in_specs, out_specs=out_specs, check_vma=False)
```

```python
import jax
import jax.numpy as jnp
from jax import lax
from jax.experimental import pallas as pl
from jax.experimental.pallas import tpu as pltpu
from jax.sharding import PartitionSpec as P

MEETINGS = 4

SCORE_SCALE = 0.1875
LR_EMBED = 0.5
LR_RELATION = 0.02

MESH = pl.DeviceIdType.MESH
F32 = jnp.float32
BF16 = jnp.bfloat16

ROW_CHUNKS = 4
EDGE_CHUNKS = 2


def partner(index, mask):
    return index + mask * (1 - 2 * lax.rem(lax.div(index, mask), 2))


def dot(a, b, a_dim, b_dim):
    return lax.dot_general(a, b, (((a_dim,), (b_dim,)), ((), ())), preferred_element_type=F32)


def kernel(
    n_inner,
    n_group,
    left_ref,
    right_ref,
    rel_ref,
    src_ref,
    dst_ref,
    len_ref,
    left_final,
    right_final,
    rel_out,
    left_out,
    right_out,
    met0,
    met1,
    met2,
    own2,
    next3,
    picked,
    query,
    query_in1,
    query_in2,
    grads,
    coeffs,
    expo,
    onehot,
    rel_own,
    src_own,
    dst_own,
    meta,
    meta_in1,
    meta_in3,
    part,
    part_in,
    shard,
    shard_in,
    gathered,
    move0_send,
    move0_recv,
    move2_send,
    move2_recv,
    move3_send,
    move3_recv,
    small_send,
    small_recv,
    ask1_send,
    ask1_recv,
    load,
    store,
    rs_send,
    rs_recv,
    ar_send,
    ar_recv,
    ag_send,
    ag_recv,
):
    me = lax.axis_index("inner")
    my_group = lax.axis_index("group")
    rows, _ = left_ref.shape
    slots = src_ref.shape[2]
    log_inner = n_inner.bit_length() - 1
    masks = [2 ** (m % log_inner) for m in range(MEETINGS)]
    first = partner(me, masks[0])
    second = partner(me, masks[1])
    third = partner(second, masks[2])
    fourth = partner(me, masks[3])
    chunk = rows // ROW_CHUNKS
    width = slots // EDGE_CHUNKS

    def inner_id(index):
        return (my_group, index)

    def group_id(index):
        return (index, me)

    def remote(src, dst, send, recv, device):
        return pltpu.make_async_remote_copy(
            src_ref=src, dst_ref=dst, send_sem=send, recv_sem=recv, device_id=device, device_id_type=MESH
        )

    def piece(i):
        return pl.ds(i * chunk, chunk)

    loads = [
        pltpu.make_async_copy(src, dst, load.at[i])
        for i, (src, dst) in enumerate(
            [(dst_ref, dst_own), (src_ref, src_own), (left_ref, left_out), (rel_ref, rel_own)]
        )
    ]
    for copy in loads:
        copy.start()

    barrier = pltpu.get_barrier_semaphore()
    for step in range(1, n_inner):
        pl.semaphore_signal(
            barrier, inc=1, device_id=inner_id(lax.rem(me + step, n_inner)), device_id_type=MESH
        )
    for step in range(1, n_group):
        pl.semaphore_signal(
            barrier, inc=1, device_id=group_id(lax.rem(my_group + step, n_group)), device_id_type=MESH
        )
    pl.semaphore_wait(barrier, n_inner + n_group - 2)

    move0 = [
        remote(right_ref.at[piece(i)], met0.at[piece(i)], move0_send.at[i], move0_recv.at[i], inner_id(first))
        for i in range(ROW_CHUNKS)
    ]
    for copy in move0:
        copy.start()

    for copy in loads:
        copy.wait()

    slot_ids = lax.broadcasted_iota(jnp.int32, (1, slots), 1)
    meta[...] = jnp.zeros_like(meta)
    for m in range(MEETINGS):
        meta[m : m + 1, :] = jnp.where(slot_ids < len_ref[0:1, m : m + 1], dst_own[0, m : m + 1, :], -1)
    meta1 = remote(meta, meta_in1, small_send.at[0], small_recv.at[0], inner_id(second))
    meta3 = remote(meta, meta_in3, small_send.at[1], small_recv.at[1], inner_id(fourth))
    meta1.start()
    meta3.start()

    entity = lax.broadcasted_iota(jnp.int32, (chunk, slots), 0)
    every = slice(0, slots)
    halves = [slice(i * width, (i + 1) * width) for i in range(EDGE_CHUNKS)]

    def make_onehot(m):
        for i in range(ROW_CHUNKS):
            hot = entity == src_own[0, m : m + 1, :] - i * chunk
            onehot[m, piece(i), :] = hot.astype(F32).astype(BF16)

    def make_queries(m, cols):
        chosen = dot(left_out[...], onehot[m, :, cols], 0, 0).astype(BF16)
        picked[m, :, cols] = chosen
        query[m, :, cols] = dot(rel_own[...], chosen, 0, 0).astype(BF16)

    def score_piece(holding, asked, buffer, i, cols):
        scores = dot(holding, asked, 1, 0) * SCORE_SCALE
        top = jnp.max(scores, axis=0, keepdims=True)
        expos = jnp.exp(scores - top)
        expo[buffer, piece(i), cols] = expos
        return top, jnp.sum(expos, axis=0, keepdims=True)

    def finish_coeffs(stats, targets, buffer, cols):
        top = stats[0][0]
        for piece_top, _ in stats[1:]:
            top = jnp.maximum(top, piece_top)
        factors = [jnp.exp(piece_top - top) for piece_top, _ in stats]
        whole = sum(factor * piece_sum for factor, (_, piece_sum) in zip(factors, stats))
        inverse = (targets >= 0).astype(F32) / whole
        for i, factor in enumerate(factors):
            weight = expo[buffer, piece(i), cols] * (factor * inverse)
            hit = entity[:, cols] == targets - i * chunk
            coeffs[piece(i), cols] = jnp.where(hit, weight - 1.0, weight).astype(BF16)

    def make_grad(m, holding):
        grads[m] = (dot(holding, coeffs[...], 0, 0) * SCORE_SCALE).astype(BF16)

    def held_update(holding, asked, i):
        held_grad = dot(coeffs[piece(i), :], asked, 1, 1) * SCORE_SCALE
        return (holding.astype(F32) - LR_EMBED * held_grad).astype(BF16)

    def left_update(m):
        row_grad = dot(rel_own[...], grads[m], 1, 0).astype(BF16)
        for i in range(ROW_CHUNKS):
            left_grad = dot(onehot[m, piece(i), :], row_grad, 1, 1)
            left_out[piece(i), :] = (left_out[piece(i), :].astype(F32) - LR_EMBED * left_grad).astype(BF16)

    def relation_grad(m):
        return dot(picked[m], grads[m], 1, 1)

    make_onehot(0)
    make_queries(0, every)
    for m in range(1, MEETINGS):
        make_onehot(m)
    stats = []
    for i in range(ROW_CHUNKS):
        move0[i].wait()
        stats.append(score_piece(met0[piece(i), :], query[0], 0, i, every))
    finish_coeffs(stats, meta[0:1, :], 0, every)
    make_grad(0, met0[...])
    left_update(0)
    ask1 = [
        remote(
            query.at[1, :, cols], query_in1.at[:, cols], ask1_send.at[i], ask1_recv.at[i], inner_id(second)
        )
        for i, cols in enumerate(halves)
    ]
    for i, cols in enumerate(halves):
        make_queries(1, cols)
        ask1[i].start()
    for i in range(ROW_CHUNKS):
        met1[piece(i), :] = held_update(met0[piece(i), :], query[0], i)
    total = relation_grad(0)

    meta1.wait()
    for half, cols in enumerate(halves):
        ask1[half].wait()
        stats = [
            score_piece(met1[piece(i), :], query_in1[:, cols], 0, i, cols) for i in range(ROW_CHUNKS)
        ]
        finish_coeffs(stats, meta_in1[1:2, cols], 0, cols)
    move2 = [
        remote(met2.at[piece(i)], own2.at[piece(i)], move2_send.at[i], move2_recv.at[i], inner_id(third))
        for i in range(ROW_CHUNKS)
    ]
    back1 = remote(grads.at[MEETINGS], grads.at[1], small_send.at[3], small_recv.at[3], inner_id(second))
    for i in range(ROW_CHUNKS):
        if i == ROW_CHUNKS // 2:
            make_grad(MEETINGS, met1[...])
            back1.start()
        met2[piece(i), :] = held_update(met1[piece(i), :], query_in1[...], i)
        move2[i].start()
    back1.wait()
    left_update(1)

    make_queries(2, every)
    ask2 = remote(query.at[2], query_in2, small_send.at[4], small_recv.at[4], inner_id(fourth))
    ask2.start()
    total = total + relation_grad(1)
    move3 = [
        remote(own2.at[piece(i)], next3.at[piece(i)], move3_send.at[i], move3_recv.at[i], inner_id(fourth))
        for i in range(ROW_CHUNKS)
    ]
    stats = []
    next_stats = []

    def score_next(i):
        move3[i].wait()
        next_stats.append(score_piece(next3[piece(i), :], query_in2[...], 1, i, every))

    for i in range(ROW_CHUNKS):
        move2[i].wait()
        move3[i].start()
        stats.append(score_piece(own2[piece(i), :], query[2], 0, i, every))
        if i == 1:
            meta3.wait()
            ask2.wait()
        if i > 0:
            score_next(i - 1)
    finish_coeffs(stats, meta[2:3, :], 0, every)
    make_grad(2, own2[...])
    left_update(2)
    make_queries(3, every)
    total = total + relation_grad(2)
    score_next(ROW_CHUNKS - 1)
    finish_coeffs(next_stats, meta_in3[2:3, :], 1, every)

    stats = []
    for i in range(ROW_CHUNKS):
        right_out[piece(i), :] = held_update(next3[piece(i), :], query_in2[...], i)
        stats.append(score_piece(right_out[piece(i), :], query[3], 0, i, every))
    finish_coeffs(stats, meta[3:4, :], 0, every)
    make_grad(3, right_out[...])
    total = total + relation_grad(3)

    share = rel_ref.shape[0] // n_inner
    for i in range(n_inner):
        part[i] = total[i * share : (i + 1) * share, :].astype(BF16)
    scatter = []
    for step in range(1, n_inner):
        to = lax.rem(me + step, n_inner)
        copy = remote(
            part.at[to], part_in.at[step - 1], rs_send.at[step - 1], rs_recv.at[step - 1], inner_id(to)
        )
        copy.start()
        scatter.append(copy)
    for i in range(ROW_CHUNKS):
        right_out[piece(i), :] = held_update(right_out[piece(i), :], query[3], i)
    left_update(3)
    stores = [
        pltpu.make_async_copy(right_out, right_final, store.at[0]),
        pltpu.make_async_copy(left_out, left_final, store.at[1]),
    ]
    for copy in stores:
        copy.start()
    own = part[me].astype(F32)
    for step, copy in enumerate(scatter):
        copy.wait()
        own = own + part_in[step].astype(F32)
    shard[...] = own
    everyone = []
    for step in range(1, n_group):
        to = lax.rem(my_group + step, n_group)
        copy = remote(
            shard, shard_in.at[my_group], ar_send.at[step - 1], ar_recv.at[step - 1], group_id(to)
        )
        copy.start()
        everyone.append(copy)
    shard_in[my_group] = own
    for copy in everyone:
        copy.wait()
    whole = shard_in[0]
    for g in range(1, n_group):
        whole = whole + shard_in[g]
    gathered[me] = whole.astype(BF16)
    spread = []
    for step in range(1, n_inner):
        to = lax.rem(me + step, n_inner)
        copy = remote(
            gathered.at[me], gathered.at[me], ag_send.at[step - 1], ag_recv.at[step - 1], inner_id(to)
        )
        copy.start()
        spread.append(copy)
    for copy in spread:
        copy.wait()
    for i in range(n_inner):
        here = slice(i * share, (i + 1) * share)
        rel_out[here, :] = rel_own[here, :].astype(F32) - LR_RELATION * gathered[i].astype(F32)
    for copy in stores:
        copy.wait()


def shards(left_part, right_part, relation, src_index, dst_index, lengths):
    n_inner = lax.axis_size("inner")
    n_group = lax.axis_size("group")
    rows, depth = left_part.shape
    slots = src_index.shape[2]
    share = depth // n_inner
    block = pltpu.VMEM((rows, depth), BF16)
    asked = pltpu.VMEM((depth, slots), BF16)
    meta = pltpu.VMEM((2 * MEETINGS, slots), jnp.int32)
    dma = pltpu.SemaphoreType.DMA
    vmem = pl.BlockSpec(memory_space=pltpu.VMEM)
    hbm = pl.BlockSpec(memory_space=pltpu.HBM)

    def body(*refs):
        kernel(n_inner, n_group, *refs)

    return pl.pallas_call(
        body,
        out_shape=(
            jax.ShapeDtypeStruct((rows, depth), BF16),
            jax.ShapeDtypeStruct((rows, depth), BF16),
            jax.ShapeDtypeStruct((depth, depth), F32),
        ),
        in_specs=[hbm] * 5 + [vmem],
        out_specs=(hbm, hbm, vmem),
        scratch_shapes=[
            block,
            block,
            block,
            block,
            block,
            block,
            block,
            pltpu.VMEM((MEETINGS, depth, slots), BF16),
            pltpu.VMEM((MEETINGS, depth, slots), BF16),
            asked,
            asked,
            pltpu.VMEM((MEETINGS + 1, depth, slots), BF16),
            pltpu.VMEM((rows, slots), BF16),
            pltpu.VMEM((2, rows, slots), F32),
            pltpu.VMEM((MEETINGS, rows, slots), BF16),
            pltpu.VMEM(relation.shape, BF16),
            pltpu.VMEM(src_index.shape, jnp.int32),
            pltpu.VMEM(dst_index.shape, jnp.int32),
            meta,
            meta,
            meta,
            pltpu.VMEM((n_inner, share, depth), BF16),
            pltpu.VMEM((n_inner - 1, share, depth), BF16),
            pltpu.VMEM((share, depth), F32),
            pltpu.VMEM((n_group, share, depth), F32),
            pltpu.VMEM((n_inner, share, depth), BF16),
            dma((ROW_CHUNKS,)),
            dma((ROW_CHUNKS,)),
            dma((ROW_CHUNKS,)),
            dma((ROW_CHUNKS,)),
            dma((ROW_CHUNKS,)),
            dma((ROW_CHUNKS,)),
            dma((5,)),
            dma((5,)),
            dma((EDGE_CHUNKS,)),
            dma((EDGE_CHUNKS,)),
            dma((4,)),
            dma((2,)),
            dma((n_inner - 1,)),
            dma((n_inner - 1,)),
            dma((n_group - 1,)),
            dma((n_group - 1,)),
            dma((n_inner - 1,)),
            dma((n_inner - 1,)),
        ],
        compiler_params=pltpu.CompilerParams(
            collective_id=0, has_side_effects=True, vmem_limit_bytes=64 * 1024 * 1024 - 512 * 1024
        ),
        cost_estimate=pl.CostEstimate(
            flops=MEETINGS * 12 * rows * slots * depth,
            bytes_accessed=8 * rows * depth,
            transcendentals=MEETINGS * rows * slots,
        ),
        name="bucket_meetings",
    )(left_part, right_part, relation, src_index, dst_index, lengths)


def solution(mesh):
    in_specs = (
        P(("group", "inner"), None),
        P(("group", "inner"), None),
        P(),
        P(("group", "inner"), None, None),
        P(("group", "inner"), None, None),
        P(("group", "inner"), None),
    )
    out_specs = (P(("group", "inner"), None), P(("group", "inner"), None), P())
    return jax.shard_map(shards, mesh=mesh, in_specs=in_specs, out_specs=out_specs, check_vma=False)
```

```python
import jax
import jax.numpy as jnp
from jax import lax
from jax.experimental import pallas as pl
from jax.experimental.pallas import tpu as pltpu
from jax.sharding import PartitionSpec as P

MEETINGS = 4

SCORE_SCALE = 0.1875
LR_EMBED = 0.5
LR_RELATION = 0.02

MESH = pl.DeviceIdType.MESH
F32 = jnp.float32
BF16 = jnp.bfloat16

ROW_CHUNKS = 4
VMEM_LIMIT = 64 * 1024 * 1024 - 512 * 1024


def partner(index, mask):
    return index + mask * (1 - 2 * lax.rem(lax.div(index, mask), 2))


def dot(a, b, a_dim, b_dim):
    return lax.dot_general(a, b, (((a_dim,), (b_dim,)), ((), ())), preferred_element_type=F32)


def kernel(
    n_inner,
    n_group,
    left_ref,
    right_ref,
    rel_ref,
    src_ref,
    dst_ref,
    len_ref,
    left_final,
    right_final,
    rel_out,
    left_out,
    right_out,
    met0,
    next1,
    met1,
    met2,
    own2,
    next3,
    picked,
    query,
    query_in1,
    query_in2,
    grads,
    coeffs,
    expo,
    onehot,
    rel_own,
    src_own,
    dst_own,
    meta,
    meta_in1,
    meta_in3,
    part,
    part_in,
    shard,
    shard_in,
    gathered,
    move0_send,
    move0_recv,
    move2_send,
    move2_recv,
    move3_send,
    move3_recv,
    small_send,
    small_recv,
    move1_send,
    move1_recv,
    load,
    store,
    rs_send,
    rs_recv,
    ar_send,
    ar_recv,
    ag_send,
    ag_recv,
):
    me = lax.axis_index("inner")
    my_group = lax.axis_index("group")
    rows, _ = left_ref.shape
    slots = src_ref.shape[2]
    log_inner = n_inner.bit_length() - 1
    masks = [2 ** (m % log_inner) for m in range(MEETINGS)]
    first = partner(me, masks[0])
    second = partner(me, masks[1])
    third = partner(me, masks[2])
    fourth = partner(me, masks[3])
    chunk = rows // ROW_CHUNKS

    def inner_id(index):
        return (my_group, index)

    def group_id(index):
        return (index, me)

    def remote(src, dst, send, recv, device):
        return pltpu.make_async_remote_copy(
            src_ref=src, dst_ref=dst, send_sem=send, recv_sem=recv, device_id=device, device_id_type=MESH
        )

    def piece(i):
        return pl.ds(i * chunk, chunk)

    loads = [
        pltpu.make_async_copy(src, dst, load.at[i])
        for i, (src, dst) in enumerate(
            [(dst_ref, dst_own), (src_ref, src_own), (left_ref, left_out), (rel_ref, rel_own)]
        )
    ]
    for copy in loads:
        copy.start()

    barrier = pltpu.get_barrier_semaphore()
    for step in range(1, n_inner):
        pl.semaphore_signal(
            barrier, inc=1, device_id=inner_id(lax.rem(me + step, n_inner)), device_id_type=MESH
        )
    for step in range(1, n_group):
        pl.semaphore_signal(
            barrier, inc=1, device_id=group_id(lax.rem(my_group + step, n_group)), device_id_type=MESH
        )
    pl.semaphore_wait(barrier, n_inner + n_group - 2)

    move0 = [
        remote(right_ref.at[piece(i)], met0.at[piece(i)], move0_send.at[i], move0_recv.at[i], inner_id(first))
        for i in range(ROW_CHUNKS)
    ]
    for copy in move0:
        copy.start()

    for copy in loads:
        copy.wait()

    slot_ids = lax.broadcasted_iota(jnp.int32, (1, slots), 1)
    meta[...] = jnp.zeros_like(meta)
    for m in range(MEETINGS):
        meta[m : m + 1, :] = jnp.where(slot_ids < len_ref[0:1, m : m + 1], dst_own[0, m : m + 1, :], -1)
    meta1 = remote(meta, meta_in1, small_send.at[0], small_recv.at[0], inner_id(second))
    meta3 = remote(meta, meta_in3, small_send.at[1], small_recv.at[1], inner_id(fourth))
    meta1.start()
    meta3.start()

    entity = lax.broadcasted_iota(jnp.int32, (chunk, slots), 0)
    every = slice(0, slots)

    def make_onehot(m):
        for i in range(ROW_CHUNKS):
            hot = entity == src_own[0, m : m + 1, :] - i * chunk
            onehot[m, piece(i), :] = hot.astype(F32).astype(BF16)

    def make_queries(m, cols):
        chosen = dot(left_out[...], onehot[m, :, cols], 0, 0).astype(BF16)
        picked[m, :, cols] = chosen
        query[m, :, cols] = dot(rel_own[...], chosen, 0, 0).astype(BF16)

    def score_piece(holding, asked, buffer, i, cols):
        scores = dot(holding, asked, 1, 0) * SCORE_SCALE
        top = jnp.max(scores, axis=0, keepdims=True)
        expos = jnp.exp(scores - top)
        expo[buffer, piece(i), cols] = expos
        return top, jnp.sum(expos, axis=0, keepdims=True)

    def finish_coeffs(stats, targets, buffer, cols):
        top = stats[0][0]
        for piece_top, _ in stats[1:]:
            top = jnp.maximum(top, piece_top)
        factors = [jnp.exp(piece_top - top) for piece_top, _ in stats]
        whole = sum(factor * piece_sum for factor, (_, piece_sum) in zip(factors, stats))
        inverse = (targets >= 0).astype(F32) / whole
        for i, factor in enumerate(factors):
            weight = expo[buffer, piece(i), cols] * (factor * inverse)
            hit = entity[:, cols] == targets - i * chunk
            coeffs[piece(i), cols] = jnp.where(hit, weight - 1.0, weight).astype(BF16)

    def make_grad(m, holding):
        grads[m] = (dot(holding, coeffs[...], 0, 0) * SCORE_SCALE).astype(BF16)

    def held_update(holding, asked, i):
        held_grad = dot(coeffs[piece(i), :], asked, 1, 1) * SCORE_SCALE
        return (holding.astype(F32) - LR_EMBED * held_grad).astype(BF16)

    def left_update(m):
        row_grad = dot(rel_own[...], grads[m], 1, 0).astype(BF16)
        for i in range(ROW_CHUNKS):
            left_grad = dot(onehot[m, piece(i), :], row_grad, 1, 1)
            left_out[piece(i), :] = (left_out[piece(i), :].astype(F32) - LR_EMBED * left_grad).astype(BF16)

    def relation_grad(m):
        return dot(picked[m], grads[m], 1, 1)

    def paired(m, moves, passes, ask, own, after, asked, notice, their_targets, result):
        stats, after_stats = [], []

        def score_after(i):
            passes[i].wait()
            after_stats.append(score_piece(after[piece(i), :], asked[...], 1, i, every))

        for i in range(ROW_CHUNKS):
            moves[i].wait()
            passes[i].start()
            stats.append(score_piece(own[piece(i), :], query[m], 0, i, every))
            if i == 1:
                notice.wait()
                ask.wait()
            if i > 0:
                score_after(i - 1)
        finish_coeffs(stats, meta[m : m + 1, :], 0, every)
        make_grad(m, own[...])
        left_update(m)
        make_queries(m + 1, every)
        grad_sum = relation_grad(m)
        score_after(ROW_CHUNKS - 1)
        finish_coeffs(after_stats, their_targets[m : m + 1, :], 1, every)
        stats = []
        for i in range(ROW_CHUNKS):
            result[piece(i), :] = held_update(after[piece(i), :], asked[...], i)
            stats.append(score_piece(result[piece(i), :], query[m + 1], 0, i, every))
        finish_coeffs(stats, meta[m + 1 : m + 2, :], 0, every)
        return grad_sum

    make_onehot(0)
    make_queries(0, every)
    ask0 = remote(query.at[0], query_in1, small_send.at[2], small_recv.at[2], inner_id(second))
    ask0.start()
    for m in range(1, MEETINGS):
        make_onehot(m)
    move1 = [
        remote(met0.at[piece(i)], next1.at[piece(i)], move1_send.at[i], move1_recv.at[i], inner_id(second))
        for i in range(ROW_CHUNKS)
    ]
    total = paired(0, move0, move1, ask0, met0, next1, query_in1, meta1, meta_in1, met1)
    move2 = [
        remote(met2.at[piece(i)], own2.at[piece(i)], move2_send.at[i], move2_recv.at[i], inner_id(third))
        for i in range(ROW_CHUNKS)
    ]
    for i in range(ROW_CHUNKS):
        met2[piece(i), :] = held_update(met1[piece(i), :], query[1], i)
        move2[i].start()
    make_grad(1, met1[...])
    left_update(1)

    make_queries(2, every)
    ask2 = remote(query.at[2], query_in2, small_send.at[3], small_recv.at[3], inner_id(fourth))
    ask2.start()
    total = total + relation_grad(1)
    move3 = [
        remote(own2.at[piece(i)], next3.at[piece(i)], move3_send.at[i], move3_recv.at[i], inner_id(fourth))
        for i in range(ROW_CHUNKS)
    ]
    total = total + paired(2, move2, move3, ask2, own2, next3, query_in2, meta3, meta_in3, right_out)
    make_grad(3, right_out[...])
    total = total + relation_grad(3)

    share = rel_ref.shape[0] // n_inner
    for i in range(n_inner):
        part[i] = total[i * share : (i + 1) * share, :].astype(BF16)
    scatter = []
    for step in range(1, n_inner):
        to = lax.rem(me + step, n_inner)
        copy = remote(
            part.at[to], part_in.at[step - 1], rs_send.at[step - 1], rs_recv.at[step - 1], inner_id(to)
        )
        copy.start()
        scatter.append(copy)
    for i in range(ROW_CHUNKS):
        right_out[piece(i), :] = held_update(right_out[piece(i), :], query[3], i)
    left_update(3)
    stores = [
        pltpu.make_async_copy(right_out, right_final, store.at[0]),
        pltpu.make_async_copy(left_out, left_final, store.at[1]),
    ]
    for copy in stores:
        copy.start()
    own = part[me].astype(F32)
    for step, copy in enumerate(scatter):
        copy.wait()
        own = own + part_in[step].astype(F32)
    shard[...] = own
    everyone = []
    for step in range(1, n_group):
        to = lax.rem(my_group + step, n_group)
        copy = remote(
            shard, shard_in.at[my_group], ar_send.at[step - 1], ar_recv.at[step - 1], group_id(to)
        )
        copy.start()
        everyone.append(copy)
    shard_in[my_group] = own
    for copy in everyone:
        copy.wait()
    whole = shard_in[0]
    for g in range(1, n_group):
        whole = whole + shard_in[g]
    gathered[me] = whole.astype(BF16)
    spread = []
    for step in range(1, n_inner):
        to = lax.rem(me + step, n_inner)
        copy = remote(
            gathered.at[me], gathered.at[me], ag_send.at[step - 1], ag_recv.at[step - 1], inner_id(to)
        )
        copy.start()
        spread.append(copy)
    for copy in spread:
        copy.wait()
    for i in range(n_inner):
        here = slice(i * share, (i + 1) * share)
        rel_out[here, :] = rel_own[here, :].astype(F32) - LR_RELATION * gathered[i].astype(F32)
    for copy in stores:
        copy.wait()


def shards(left_part, right_part, relation, src_index, dst_index, lengths):
    n_inner = lax.axis_size("inner")
    n_group = lax.axis_size("group")
    rows, depth = left_part.shape
    slots = src_index.shape[2]
    share = depth // n_inner
    block = pltpu.VMEM((rows, depth), BF16)
    asked = pltpu.VMEM((depth, slots), BF16)
    meta = pltpu.VMEM((2 * MEETINGS, slots), jnp.int32)
    dma = pltpu.SemaphoreType.DMA
    vmem = pl.BlockSpec(memory_space=pltpu.VMEM)
    hbm = pl.BlockSpec(memory_space=pltpu.HBM)

    def body(*refs):
        kernel(n_inner, n_group, *refs)

    results = pl.pallas_call(
        body,
        out_shape=(
            jax.ShapeDtypeStruct((rows, depth), BF16),
            jax.ShapeDtypeStruct((rows, depth), BF16),
            jax.ShapeDtypeStruct((depth, depth), F32),
        ),
        in_specs=[hbm] * 5 + [vmem],
        out_specs=(hbm, hbm, vmem),
        scratch_shapes=[
            block,
            block,
            block,
            block,
            block,
            block,
            block,
            block,
            pltpu.VMEM((MEETINGS, depth, slots), BF16),
            pltpu.VMEM((MEETINGS, depth, slots), BF16),
            asked,
            asked,
            pltpu.VMEM((MEETINGS, depth, slots), BF16),
            pltpu.VMEM((rows, slots), BF16),
            pltpu.VMEM((2, rows, slots), F32),
            pltpu.VMEM((MEETINGS, rows, slots), BF16),
            pltpu.VMEM(relation.shape, BF16),
            pltpu.VMEM(src_index.shape, jnp.int32),
            pltpu.VMEM(dst_index.shape, jnp.int32),
            meta,
            meta,
            meta,
            pltpu.VMEM((n_inner, share, depth), BF16),
            pltpu.VMEM((n_inner - 1, share, depth), BF16),
            pltpu.VMEM((share, depth), F32),
            pltpu.VMEM((n_group, share, depth), F32),
            pltpu.VMEM((n_inner, share, depth), BF16),
            dma((ROW_CHUNKS,)),
            dma((ROW_CHUNKS,)),
            dma((ROW_CHUNKS,)),
            dma((ROW_CHUNKS,)),
            dma((ROW_CHUNKS,)),
            dma((ROW_CHUNKS,)),
            dma((4,)),
            dma((4,)),
            dma((ROW_CHUNKS,)),
            dma((ROW_CHUNKS,)),
            dma((4,)),
            dma((2,)),
            dma((n_inner - 1,)),
            dma((n_inner - 1,)),
            dma((n_group - 1,)),
            dma((n_group - 1,)),
            dma((n_inner - 1,)),
            dma((n_inner - 1,)),
        ],
        compiler_params=pltpu.CompilerParams(
            collective_id=0, has_side_effects=True, vmem_limit_bytes=VMEM_LIMIT
        ),
        cost_estimate=pl.CostEstimate(
            flops=MEETINGS * 12 * rows * slots * depth,
            bytes_accessed=8 * rows * depth,
            transcendentals=MEETINGS * rows * slots,
        ),
        name="bucket_meetings",
    )(left_part, right_part, relation, src_index, dst_index, lengths)

    def hand_out(*refs):
        sems = refs[-1]
        copies = []
        for source, target in zip(refs[:3], refs[3:6]):
            height = source.shape[0] // ROW_CHUNKS
            for i in range(ROW_CHUNKS):
                here = pl.ds(i * height, height)
                copies.append(pltpu.make_async_copy(source.at[here], target.at[here], sems.at[len(copies)]))
        for copy in copies:
            copy.start()
        for copy in copies:
            copy.wait()

    return pl.pallas_call(
        hand_out,
        out_shape=tuple(jax.ShapeDtypeStruct(r.shape, r.dtype) for r in results),
        in_specs=[hbm] * 3,
        out_specs=(hbm,) * 3,
        scratch_shapes=[dma((3 * ROW_CHUNKS,))],
        compiler_params=pltpu.CompilerParams(vmem_limit_bytes=VMEM_LIMIT),
        name="hand_out",
    )(*results)


def solution(mesh):
    in_specs = (
        P(("group", "inner"), None),
        P(("group", "inner"), None),
        P(),
        P(("group", "inner"), None, None),
        P(("group", "inner"), None, None),
        P(("group", "inner"), None),
    )
    out_specs = (P(("group", "inner"), None), P(("group", "inner"), None), P())
    return jax.shard_map(shards, mesh=mesh, in_specs=in_specs, out_specs=out_specs, check_vma=False)
```

```python
import jax
import jax.numpy as jnp
from jax import lax
from jax.experimental import pallas as pl
from jax.experimental.pallas import tpu as pltpu
from jax.sharding import PartitionSpec as P

MEETINGS = 4

SCORE_SCALE = 0.1875
LR_EMBED = 0.5
LR_RELATION = 0.02

MESH = pl.DeviceIdType.MESH
F32 = jnp.float32
BF16 = jnp.bfloat16

ROW_CHUNKS = 4
VMEM_LIMIT = 64 * 1024 * 1024 - 512 * 1024


def partner(index, mask):
    return index + mask * (1 - 2 * lax.rem(lax.div(index, mask), 2))


def dot(a, b, a_dim, b_dim):
    return lax.dot_general(a, b, (((a_dim,), (b_dim,)), ((), ())), preferred_element_type=F32)


def kernel(
    n_inner,
    n_group,
    left_ref,
    right_ref,
    rel_ref,
    src_ref,
    dst_ref,
    len_ref,
    left_final,
    right_final,
    rel_out,
    left_out,
    right_out,
    met0,
    next1,
    met1,
    met2,
    own2,
    next3,
    picked,
    query,
    query_in1,
    query_in2,
    grads,
    coeffs,
    expo,
    onehot,
    rel_own,
    src_own,
    dst_own,
    meta,
    meta_in1,
    meta_in3,
    part,
    part_in,
    shard,
    shard_in,
    gathered,
    move0_send,
    move0_recv,
    move2_send,
    move2_recv,
    move3_send,
    move3_recv,
    small_send,
    small_recv,
    move1_send,
    move1_recv,
    load,
    store,
    rs_send,
    rs_recv,
    ar_send,
    ar_recv,
    ag_send,
    ag_recv,
):
    me = lax.axis_index("inner")
    my_group = lax.axis_index("group")
    rows, _ = left_ref.shape
    slots = src_ref.shape[2]
    log_inner = n_inner.bit_length() - 1
    masks = [2 ** (m % log_inner) for m in range(MEETINGS)]
    first = partner(me, masks[0])
    second = partner(me, masks[1])
    third = partner(me, masks[2])
    fourth = partner(me, masks[3])
    chunk = rows // ROW_CHUNKS

    def inner_id(index):
        return (my_group, index)

    def group_id(index):
        return (index, me)

    def remote(src, dst, send, recv, device):
        return pltpu.make_async_remote_copy(
            src_ref=src, dst_ref=dst, send_sem=send, recv_sem=recv, device_id=device, device_id_type=MESH
        )

    def piece(i):
        return pl.ds(i * chunk, chunk)

    loads = [
        pltpu.make_async_copy(src, dst, load.at[i])
        for i, (src, dst) in enumerate(
            [(dst_ref, dst_own), (src_ref, src_own), (left_ref, left_out), (rel_ref, rel_own)]
        )
    ]
    for copy in loads:
        copy.start()

    barrier = pltpu.get_barrier_semaphore()
    for step in range(1, n_inner):
        pl.semaphore_signal(
            barrier, inc=1, device_id=inner_id(lax.rem(me + step, n_inner)), device_id_type=MESH
        )
    for step in range(1, n_group):
        pl.semaphore_signal(
            barrier, inc=1, device_id=group_id(lax.rem(my_group + step, n_group)), device_id_type=MESH
        )
    pl.semaphore_wait(barrier, n_inner + n_group - 2)

    move0 = [
        remote(right_ref.at[piece(i)], met0.at[piece(i)], move0_send.at[i], move0_recv.at[i], inner_id(first))
        for i in range(ROW_CHUNKS)
    ]
    for copy in move0:
        copy.start()

    for copy in loads:
        copy.wait()

    slot_ids = lax.broadcasted_iota(jnp.int32, (1, slots), 1)
    meta[...] = jnp.zeros_like(meta)
    for m in range(MEETINGS):
        meta[m : m + 1, :] = jnp.where(slot_ids < len_ref[0:1, m : m + 1], dst_own[0, m : m + 1, :], -1)
    meta1 = remote(meta, meta_in1, small_send.at[0], small_recv.at[0], inner_id(second))
    meta3 = remote(meta, meta_in3, small_send.at[1], small_recv.at[1], inner_id(fourth))
    meta1.start()
    meta3.start()

    entity = lax.broadcasted_iota(jnp.int32, (chunk, slots), 0)
    every = slice(0, slots)

    def make_onehot(m):
        for i in range(ROW_CHUNKS):
            hot = entity == src_own[0, m : m + 1, :] - i * chunk
            onehot[m, piece(i), :] = hot.astype(F32).astype(BF16)

    def make_queries(m, cols):
        chosen = dot(left_out[...], onehot[m, :, cols], 0, 0).astype(BF16)
        picked[m, :, cols] = chosen
        query[m, :, cols] = dot(rel_own[...], chosen, 0, 0).astype(BF16)

    def score_piece(holding, asked, buffer, i, cols):
        scores = dot(holding, asked, 1, 0) * SCORE_SCALE
        top = jnp.max(scores, axis=0, keepdims=True)
        expos = jnp.exp(scores - top)
        expo[buffer, piece(i), cols] = expos
        return top, jnp.sum(expos, axis=0, keepdims=True)

    def finish_coeffs(stats, targets, buffer, cols):
        top = stats[0][0]
        for piece_top, _ in stats[1:]:
            top = jnp.maximum(top, piece_top)
        factors = [jnp.exp(piece_top - top) for piece_top, _ in stats]
        whole = sum(factor * piece_sum for factor, (_, piece_sum) in zip(factors, stats))
        inverse = (targets >= 0).astype(F32) / whole
        for i, factor in enumerate(factors):
            weight = expo[buffer, piece(i), cols] * (factor * inverse)
            hit = entity[:, cols] == targets - i * chunk
            coeffs[piece(i), cols] = jnp.where(hit, weight - 1.0, weight).astype(BF16)

    def make_grad(m, holding):
        grads[m] = (dot(holding, coeffs[...], 0, 0) * SCORE_SCALE).astype(BF16)

    def held_update(holding, asked, i):
        held_grad = dot(coeffs[piece(i), :], asked, 1, 1) * SCORE_SCALE
        return (holding.astype(F32) - LR_EMBED * held_grad).astype(BF16)

    def left_update(m):
        row_grad = dot(rel_own[...], grads[m], 1, 0).astype(BF16)
        left_grad = dot(onehot[m], row_grad, 1, 1)
        left_out[...] = (left_out[...].astype(F32) - LR_EMBED * left_grad).astype(BF16)

    def relation_grad(m):
        return dot(picked[m], grads[m], 1, 1)

    def paired(m, moves, passes, ask, own, after, asked, notice, their_targets, result):
        stats, after_stats = [], []

        def score_after(i):
            passes[i].wait()
            after_stats.append(score_piece(after[piece(i), :], asked[...], 1, i, every))

        for i in range(ROW_CHUNKS):
            moves[i].wait()
            passes[i].start()
            stats.append(score_piece(own[piece(i), :], query[m], 0, i, every))
            if i == 1:
                notice.wait()
                ask.wait()
            if i > 0:
                score_after(i - 1)
        finish_coeffs(stats, meta[m : m + 1, :], 0, every)
        make_grad(m, own[...])
        left_update(m)
        make_queries(m + 1, every)
        grad_sum = relation_grad(m)
        score_after(ROW_CHUNKS - 1)
        finish_coeffs(after_stats, their_targets[m : m + 1, :], 1, every)
        stats = []
        for i in range(ROW_CHUNKS):
            result[piece(i), :] = held_update(after[piece(i), :], asked[...], i)
            stats.append(score_piece(result[piece(i), :], query[m + 1], 0, i, every))
        finish_coeffs(stats, meta[m + 1 : m + 2, :], 0, every)
        return grad_sum

    make_onehot(0)
    make_queries(0, every)
    ask0 = remote(query.at[0], query_in1, small_send.at[2], small_recv.at[2], inner_id(second))
    ask0.start()
    for m in range(1, MEETINGS):
        make_onehot(m)
    move1 = [
        remote(met0.at[piece(i)], next1.at[piece(i)], move1_send.at[i], move1_recv.at[i], inner_id(second))
        for i in range(ROW_CHUNKS)
    ]
    total = paired(0, move0, move1, ask0, met0, next1, query_in1, meta1, meta_in1, met1)
    move2 = [
        remote(met2.at[piece(i)], own2.at[piece(i)], move2_send.at[i], move2_recv.at[i], inner_id(third))
        for i in range(ROW_CHUNKS)
    ]
    for i in range(ROW_CHUNKS):
        met2[piece(i), :] = held_update(met1[piece(i), :], query[1], i)
        move2[i].start()
    make_grad(1, met1[...])
    left_update(1)

    make_queries(2, every)
    ask2 = remote(query.at[2], query_in2, small_send.at[3], small_recv.at[3], inner_id(fourth))
    ask2.start()
    total = total + relation_grad(1)
    move3 = [
        remote(own2.at[piece(i)], next3.at[piece(i)], move3_send.at[i], move3_recv.at[i], inner_id(fourth))
        for i in range(ROW_CHUNKS)
    ]
    total = total + paired(2, move2, move3, ask2, own2, next3, query_in2, meta3, meta_in3, right_out)
    make_grad(3, right_out[...])
    total = total + relation_grad(3)

    share = rel_ref.shape[0] // n_inner
    for i in range(n_inner):
        part[i] = total[i * share : (i + 1) * share, :].astype(BF16)
    scatter = []
    for step in range(1, n_inner):
        to = lax.rem(me + step, n_inner)
        copy = remote(
            part.at[to], part_in.at[step - 1], rs_send.at[step - 1], rs_recv.at[step - 1], inner_id(to)
        )
        copy.start()
        scatter.append(copy)
    for i in range(ROW_CHUNKS):
        right_out[piece(i), :] = held_update(right_out[piece(i), :], query[3], i)
    left_update(3)
    stores = [
        pltpu.make_async_copy(right_out, right_final, store.at[0]),
        pltpu.make_async_copy(left_out, left_final, store.at[1]),
    ]
    for copy in stores:
        copy.start()
    own = part[me].astype(F32)
    for step, copy in enumerate(scatter):
        copy.wait()
        own = own + part_in[step].astype(F32)
    shard[...] = own
    everyone = []
    for step in range(1, n_group):
        to = lax.rem(my_group + step, n_group)
        copy = remote(
            shard, shard_in.at[my_group], ar_send.at[step - 1], ar_recv.at[step - 1], group_id(to)
        )
        copy.start()
        everyone.append(copy)
    shard_in[my_group] = own
    for copy in everyone:
        copy.wait()
    whole = shard_in[0]
    for g in range(1, n_group):
        whole = whole + shard_in[g]
    gathered[me] = whole.astype(BF16)
    spread = []
    for step in range(1, n_inner):
        to = lax.rem(me + step, n_inner)
        copy = remote(
            gathered.at[me], gathered.at[me], ag_send.at[step - 1], ag_recv.at[step - 1], inner_id(to)
        )
        copy.start()
        spread.append(copy)
    for copy in spread:
        copy.wait()
    for i in range(n_inner):
        here = slice(i * share, (i + 1) * share)
        rel_out[here, :] = rel_own[here, :].astype(F32) - LR_RELATION * gathered[i].astype(F32)
    for copy in stores:
        copy.wait()


def shards(left_part, right_part, relation, src_index, dst_index, lengths):
    n_inner = lax.axis_size("inner")
    n_group = lax.axis_size("group")
    rows, depth = left_part.shape
    slots = src_index.shape[2]
    share = depth // n_inner
    block = pltpu.VMEM((rows, depth), BF16)
    asked = pltpu.VMEM((depth, slots), BF16)
    meta = pltpu.VMEM((2 * MEETINGS, slots), jnp.int32)
    dma = pltpu.SemaphoreType.DMA
    vmem = pl.BlockSpec(memory_space=pltpu.VMEM)
    hbm = pl.BlockSpec(memory_space=pltpu.HBM)

    def body(*refs):
        kernel(n_inner, n_group, *refs)

    results = pl.pallas_call(
        body,
        out_shape=(
            jax.ShapeDtypeStruct((rows, depth), BF16),
            jax.ShapeDtypeStruct((rows, depth), BF16),
            jax.ShapeDtypeStruct((depth, depth), F32),
        ),
        in_specs=[hbm] * 5 + [vmem],
        out_specs=(hbm, hbm, vmem),
        scratch_shapes=[
            block,
            block,
            block,
            block,
            block,
            block,
            block,
            block,
            pltpu.VMEM((MEETINGS, depth, slots), BF16),
            pltpu.VMEM((MEETINGS, depth, slots), BF16),
            asked,
            asked,
            pltpu.VMEM((MEETINGS, depth, slots), BF16),
            pltpu.VMEM((rows, slots), BF16),
            pltpu.VMEM((2, rows, slots), F32),
            pltpu.VMEM((MEETINGS, rows, slots), BF16),
            pltpu.VMEM(relation.shape, BF16),
            pltpu.VMEM(src_index.shape, jnp.int32),
            pltpu.VMEM(dst_index.shape, jnp.int32),
            meta,
            meta,
            meta,
            pltpu.VMEM((n_inner, share, depth), BF16),
            pltpu.VMEM((n_inner - 1, share, depth), BF16),
            pltpu.VMEM((share, depth), F32),
            pltpu.VMEM((n_group, share, depth), F32),
            pltpu.VMEM((n_inner, share, depth), BF16),
            dma((ROW_CHUNKS,)),
            dma((ROW_CHUNKS,)),
            dma((ROW_CHUNKS,)),
            dma((ROW_CHUNKS,)),
            dma((ROW_CHUNKS,)),
            dma((ROW_CHUNKS,)),
            dma((4,)),
            dma((4,)),
            dma((ROW_CHUNKS,)),
            dma((ROW_CHUNKS,)),
            dma((4,)),
            dma((2,)),
            dma((n_inner - 1,)),
            dma((n_inner - 1,)),
            dma((n_group - 1,)),
            dma((n_group - 1,)),
            dma((n_inner - 1,)),
            dma((n_inner - 1,)),
        ],
        compiler_params=pltpu.CompilerParams(
            collective_id=0, has_side_effects=True, vmem_limit_bytes=VMEM_LIMIT
        ),
        cost_estimate=pl.CostEstimate(
            flops=MEETINGS * 12 * rows * slots * depth,
            bytes_accessed=8 * rows * depth,
            transcendentals=MEETINGS * rows * slots,
        ),
        name="bucket_meetings",
    )(left_part, right_part, relation, src_index, dst_index, lengths)

    def hand_out(*refs):
        sources, targets, held = refs[:3], refs[3:6], refs[6:9]
        load, store = refs[9:]
        loads, stores = [], []
        for source, target, buffer in zip(sources, targets, held):
            height = source.shape[0] // ROW_CHUNKS
            for i in range(ROW_CHUNKS):
                here = pl.ds(i * height, height)
                at = len(loads)
                loads.append(pltpu.make_async_copy(source.at[here], buffer.at[here], load.at[at]))
                stores.append(pltpu.make_async_copy(buffer.at[here], target.at[here], store.at[at]))
        for copy in loads:
            copy.start()
        for loaded, copy in zip(loads, stores):
            loaded.wait()
            copy.start()
        for copy in stores:
            copy.wait()

    return pl.pallas_call(
        hand_out,
        out_shape=tuple(jax.ShapeDtypeStruct(r.shape, r.dtype) for r in results),
        in_specs=[hbm] * 3,
        out_specs=(hbm,) * 3,
        scratch_shapes=[pltpu.VMEM(r.shape, r.dtype) for r in results] + [dma((3 * ROW_CHUNKS,))] * 2,
        compiler_params=pltpu.CompilerParams(vmem_limit_bytes=VMEM_LIMIT),
        name="hand_out",
    )(*results)


def solution(mesh):
    in_specs = (
        P(("group", "inner"), None),
        P(("group", "inner"), None),
        P(),
        P(("group", "inner"), None, None),
        P(("group", "inner"), None, None),
        P(("group", "inner"), None),
    )
    out_specs = (P(("group", "inner"), None), P(("group", "inner"), None), P())
    return jax.shard_map(shards, mesh=mesh, in_specs=in_specs, out_specs=out_specs, check_vma=False)
```
